128 devices in a mesh: replica: 8 (over y_lo, x), section: 16 (over y_hi, z, core).
Axes of the slice: x: 4, y: 4 (y_hi: 2, y_lo: 2; y = y_hi * 2 + y_lo), z: 4, core: 2. Of those that a mesh axis runs over, the one named last changes fastest.
Arguments:
- inputs: bfloat16 [8, 4, 32, 4096], P('replica'), may hold values from -6 to 6
- routes: int32 [4, 15, 8], replicated, may hold values from 0 to 7, each once within a row
- weights: bfloat16 [8, 16, 4096, 512], P('replica', 'section'), may hold values from -6 to 6
- anchor: bfloat16 [8, 16, 4096, 512], P('replica', 'section'), may hold values from -6 to 6
- momentum: bfloat16 [8, 16, 4096, 512], P('replica', 'section'), may hold values from -3 to 3
- partner: int32 [8], replicated, may hold values from 0 to 7, as said below
Outputs:
- finals: bfloat16 [8, 4, 32, 4096], P('replica', None, None, 'section')
- new_weights: bfloat16 [8, 16, 4096, 512], P('replica', 'section')
- new_momentum: bfloat16 [8, 16, 4096, 512], P('replica', 'section')
The draws below stay inside these ranges and needn't reach their ends.
Inputs may be any that keep to these rules, and one draw needn't show every extreme that they name: partner pairs the replicas: partner[partner[r]] = r and partner[r] != r. Each routes[m, s] is a permutation of the replicas.
All inputs are finite; a program needn't handle non-finite values.
Results may differ from the reference program's by a relative error of at most 0.028.
Values may be sent and summed in bfloat16 or wider, within the bound.
A program may use at most 128 MiB of HBM per device.

```python
import jax
import jax.numpy as jnp
from jax import lax

D = 4096
H = 512
TMB = 32
MB = 4
REPLICAS = 8
SECTIONS = 16


def draw_partner(key, part):
    key = jax.random.fold_in(key, 11)
    order = jax.random.permutation(key, REPLICAS).astype(jnp.int32)
    evens = order[0::2]
    odds = order[1::2]
    paired = jnp.zeros((REPLICAS,), jnp.int32).at[evens].set(odds).at[odds].set(evens)
    return paired.astype(jnp.int32)


def level_of(key, dims, split, low, high):
    def one(dim, parts):
        draws = jax.random.uniform(jax.random.fold_in(jax.random.fold_in(key, 6), dim), (parts,), jnp.float32, low / len(split), high / len(split))
        return jnp.repeat(jnp.exp(draws), dims[dim] // parts).reshape((-1,) + (1,) * (len(dims) - dim - 1))

    loudness = one(*split[0])
    for cut in split[1:]:
        loudness = loudness * one(*cut)
    return loudness


def gaussian(own_key, extent, spread, bound, pieces=(), kind=jnp.bfloat16):
    entries = spread * jax.random.normal(own_key, extent, jnp.float32)
    if pieces:
        entries = entries * level_of(own_key, extent, pieces, -0.22, 0.18)
    return jnp.clip(entries, -bound, bound).astype(kind)


def setup_inputs(seed: int = 0) -> dict:
    arg_keys = jax.random.split(jax.random.key(seed), 7)
    return {
        "inputs": gaussian(arg_keys[0], (REPLICAS, MB, TMB, D), 1.0, 6.0, ((0, 8),)),
        "routes": jax.vmap(lambda own: jax.random.permutation(own, REPLICAS))(jax.random.split(arg_keys[1], MB * (SECTIONS - 1))).reshape((MB, SECTIONS - 1, REPLICAS)).astype(jnp.int32),
        "weights": gaussian(arg_keys[2], (REPLICAS, SECTIONS, D, H), 1.0, 6.0, ((0, 8), (1, 16))),
        "anchor": gaussian(arg_keys[3], (REPLICAS, SECTIONS, D, H), 1.0, 6.0, ((0, 8), (1, 16))),
        "momentum": gaussian(arg_keys[4], (REPLICAS, SECTIONS, D, H), 0.5, 3.0, ((0, 8), (1, 16))),
        "partner": draw_partner(jax.random.fold_in(arg_keys[6], 71), 0),
    }


def section_apply(activity, weight_one):
    values = activity.astype(jnp.float32)
    factor = lax.rsqrt(lax.optimization_barrier(jnp.mean(values * values, axis=-1, keepdims=True)) + 1e-05)
    normed = (values * factor).astype(jnp.bfloat16)
    before = jnp.dot(normed, weight_one, preferred_element_type=jnp.float32) * weight_one.shape[0] ** (-0.5)
    hidden = jax.nn.silu(before).astype(jnp.bfloat16)
    branch = lax.dot_general(hidden, weight_one, (((1,), (1,)), ((), ())), preferred_element_type=jnp.float32)
    branch = branch * weight_one.shape[1] ** (-0.5)
    return (values + branch).astype(jnp.bfloat16)

def apply_both(both):
    return section_apply(both[0], both[1])

def reference(inputs, routes, weights, anchor, momentum, partner):
    identity = jnp.arange(REPLICAS, dtype=jnp.int32)[None, :]
    by_section = jnp.moveaxis(weights, 1, 0)
    outputs = []
    for micro in range(MB):
        targets = jnp.concatenate([routes[micro].astype(jnp.int32), identity], axis=0)

        def advance(current, scanned):
            section_weights, destinations = scanned
            leaving = lax.map(apply_both, (current, section_weights))
            routed = jnp.zeros_like(leaving).at[destinations].set(leaving)
            return (routed, 0)
        final_states, _ = lax.scan(advance, inputs[:, micro], (by_section, targets))
        outputs.append(final_states)
    finals = jnp.stack(outputs, axis=1)
    own_weights = weights.astype(jnp.float32)
    own_momentum = momentum.astype(jnp.float32)
    mean_weights = 0.5 * (own_weights + own_weights[partner])
    mean_momentum = 0.5 * (own_momentum + own_momentum[partner])
    delta = anchor.astype(jnp.float32) - mean_weights
    momentum_next = 0.9 * mean_momentum + delta
    new_momentum = momentum_next.astype(jnp.bfloat16)
    new_weights = (anchor.astype(jnp.float32) - 0.7 * (delta + 0.9 * momentum_next)).astype(jnp.bfloat16)
    return (finals, new_weights, new_momentum)
```

```python
import functools

import jax
import jax.numpy as jnp
from jax import lax
from jax.experimental import pallas as pl
from jax.experimental.pallas import tpu as pltpu
from jax.sharding import PartitionSpec as P

MESH = pl.DeviceIdType.MESH
FAR = (6, 2, 5, 7, 4, 1, 3)
NEAR = (0, 1, 3, 4, 5, 7, 2, 6)
REPLICAS = 8
SECTIONS = 16
MICRO = 4
TOKENS = 32
WIDTH = 4096
HIDDEN = 512
SLICE = WIDTH // REPLICAS
PIECES = 8
ROWS = SLICE // PIECES
STEPS = 2 * PIECES


def other_replica(r, k):
    x, y = lax.rem(r, 4), lax.div(r, 4)
    x = (x, x + 1 - 2 * lax.rem(x, 2), lax.rem(x + 2, 4), 3 - x)[k % 4]
    y = (y, 1 - y)[k // 4]
    return y * 4 + x


def before_relay(section):
    return 2 * section


def kernel(
    inputs, routes, partner, weights, momentum,
    finals, landed, received,
    wv, wt, xbuf, obuf, first, second, fin, fin_out, stage_in, stage_out,
    w_sem, x_sem, o_sem, p1_sem, p2_sem, fin_sem, fin_send, land_sem, bulk_send, rec_sem, own_sem, stage_sem,
):
    r = lax.axis_index("replica")
    s = lax.axis_index("section")
    odd = lax.rem(s, 2)
    last = SECTIONS - 1

    load_w = pltpu.make_async_copy(weights, wv, w_sem)
    load_w.start()

    barrier = pltpu.get_barrier_semaphore()

    def greet(device):
        pl.semaphore_signal(barrier, inc=1, device_id=device, device_id_type=MESH)

    for k in range(1, 8):
        greet((other_replica(r, k), s))

    @pl.when(s > 0)
    def _():
        for k in range(8):
            greet((other_replica(r, k), s - 1))

    @pl.when(s < last - 1)
    def _():
        greet((r, last))

    pl.semaphore_wait(barrier, jnp.where(s < last, 15, 7 + last - 1))

    def slice_rows(q, piece):
        return pl.ds(pl.multiple_of(q * SLICE + piece * ROWS, ROWS), ROWS)

    def piece_rows(piece):
        return pl.ds(pl.multiple_of(piece * ROWS, ROWS), ROWS)

    def take_slices(step):
        array, piece = lax.div(step, PIECES), lax.rem(step, PIECES)
        for which, source in enumerate((weights, momentum)):

            @pl.when(array == which)
            def _():
                for k in FAR:
                    q = other_replica(r, k)
                    pltpu.make_async_remote_copy(
                        src_ref=source.at[slice_rows(q, piece)],
                        dst_ref=landed.at[which, r, piece_rows(piece)],
                        send_sem=bulk_send.at[step],
                        recv_sem=land_sem.at[step],
                        device_id=(q, s),
                        device_id_type=MESH,
                    ).start()
                pltpu.make_async_copy(
                    source.at[slice_rows(r, piece)],
                    landed.at[which, r, piece_rows(piece)],
                    land_sem.at[step],
                ).start()

    def pass_on(step):
        array, piece = lax.div(step, PIECES), lax.rem(step, PIECES)
        slot = lax.rem(step, 2)
        arrived = landed.at[array, :, piece_rows(piece)]
        pltpu.make_async_copy(arrived, arrived, land_sem.at[step]).wait()
        fetch = pltpu.make_async_copy(arrived, stage_in, stage_sem)
        fetch.start()
        fetch.wait()
        for k in FAR + (0,):
            d = other_replica(r, k)
            stage_out[slot, d] = stage_in[partner[d]]
            if k:
                pltpu.make_async_remote_copy(
                    src_ref=stage_out.at[slot, d],
                    dst_ref=received.at[array, r, piece_rows(piece)],
                    send_sem=bulk_send.at[STEPS + step],
                    recv_sem=rec_sem.at[step],
                    device_id=(d, s),
                    device_id_type=MESH,
                ).start()
            else:
                pltpu.make_async_copy(
                    stage_out.at[slot, d],
                    received.at[array, r, piece_rows(piece)],
                    own_sem.at[step],
                ).start()

    def sent(step):
        some = landed.at[0, pl.ds(0, 7), pl.ds(0, ROWS)]
        pltpu.make_async_copy(some, some, bulk_send.at[step]).wait()

        @pl.when(step >= STEPS)
        def _():
            one = stage_out.at[0, 0]
            pltpu.make_async_copy(one, one, own_sem.at[step - STEPS]).wait()

    def route(micro, way):
        whole = first.at[micro, way]
        pltpu.make_async_copy(whole, whole, p1_sem.at[micro, way]).wait()
        row = s - 1 + way
        targets = [routes[micro, row, source] for source in range(REPLICAS)]
        for k in FAR + (0,):
            d = other_replica(r, k)
            chosen = first[micro, way, 0]
            for source in range(1, REPLICAS):
                chosen = jnp.where(targets[source] == d, first[micro, way, source], chosen)
            second[micro, way, d] = chosen
            passing = functools.partial(
                pltpu.make_async_remote_copy,
                src_ref=second.at[micro, way, d],
                dst_ref=xbuf.at[micro, r],
                send_sem=p2_sem.at[micro, way],
                recv_sem=x_sem.at[micro, r],
                device_id=(d, s + way),
                device_id_type=MESH,
            )
            if k or way:
                passing().start()
            else:
                pltpu.make_async_copy(second.at[micro, way, d], xbuf.at[micro, r], x_sem.at[micro, r]).start()

    def apply_section(micro):
        before = jnp.zeros((TOKENS, HIDDEN), jnp.float32)
        squares = jnp.zeros((TOKENS, 128), jnp.float32)
        for k in NEAR:
            q = other_replica(r, k)
            here = xbuf.at[micro, q]
            pltpu.make_async_copy(here, here, x_sem.at[micro, q]).wait()
            block = xbuf[micro, q]
            rows = pl.ds(pl.multiple_of(q * SLICE, SLICE), SLICE)
            before = before + jnp.dot(block, wv[rows, :], preferred_element_type=jnp.float32)
            values = block.astype(jnp.float32)
            values = values * values
            for c in range(SLICE // 128):
                squares = squares + values[:, c * 128 : (c + 1) * 128]
        factor = lax.rsqrt(jnp.sum(squares, axis=-1, keepdims=True) * (1.0 / WIDTH) + 1e-05)
        before = before * (factor * WIDTH ** (-0.5))
        hidden = jax.nn.silu(before).astype(jnp.bfloat16)

        def leaving(q):
            columns = pl.ds(pl.multiple_of(q * SLICE, SLICE), SLICE)
            branch = jnp.dot(hidden, wt[:, columns], preferred_element_type=jnp.float32)
            return (xbuf[micro, q].astype(jnp.float32) + branch * HIDDEN ** (-0.5)).astype(jnp.bfloat16)

        @pl.when(s < last)
        def _():
            for k in FAR + (0,):
                q = other_replica(r, k)
                obuf[micro, q] = leaving(q)
                remote = pltpu.make_async_remote_copy(
                    src_ref=obuf.at[micro, q],
                    dst_ref=first.at[micro, odd, r],
                    send_sem=o_sem.at[micro],
                    recv_sem=p1_sem.at[micro, odd],
                    device_id=(q, s + 1 - odd),
                    device_id_type=MESH,
                )
                if k:
                    remote.start()
                else:
                    pl.when(odd == 0)(remote.start)

                    @pl.when(odd == 1)
                    def _():
                        pltpu.make_async_copy(
                            obuf.at[micro, q], first.at[micro, 1, r], p1_sem.at[micro, 1]
                        ).start()

        @pl.when(s == last)
        def _():
            half = SLICE // 2
            for q in range(REPLICAS):
                block = leaving(q)
                for side in range(2):
                    section = 2 * q + side
                    fin_out[micro, section] = block[:, side * half : (side + 1) * half]
                    if section < last:
                        pltpu.make_async_remote_copy(
                            src_ref=fin_out.at[micro, section],
                            dst_ref=fin.at[micro],
                            send_sem=fin_send.at[micro],
                            recv_sem=fin_sem.at[micro],
                            device_id=(r, section),
                            device_id_type=MESH,
                        ).start()
                    else:
                        pltpu.make_async_copy(
                            fin_out.at[micro, section], fin.at[micro], fin_sem.at[micro]
                        ).start()

    def relay():
        def turn(t, carry):
            @pl.when((odd == 1) & (t < MICRO))
            def _():
                route(t, 0)

            @pl.when((t >= 1) & (t < MICRO + 1))
            def _():
                apply_section(t - 1)

            @pl.when((odd == 1) & (s < last) & (t >= 2))
            def _():
                route(t - 2, 1)

            return carry

        lax.fori_loop(0, MICRO + 2, turn, 0)

    @pl.when(s == 0)
    def _():
        for micro in range(MICRO):
            for q in range(REPLICAS):
                pltpu.make_async_copy(
                    inputs.at[micro, :, pl.ds(q * SLICE, SLICE)], xbuf.at[micro, q], x_sem.at[micro, q]
                ).start()

    load_w.wait()
    wt[...] = wv[...].T

    ahead = before_relay(s)

    def exchange(t, carry):
        pl.when(t == ahead)(relay)

        @pl.when(t >= 2)
        def _():
            sent(t - 2)

        @pl.when(t < STEPS)
        def _():
            take_slices(t)

        @pl.when(t >= STEPS)
        def _():
            pass_on(t - STEPS)

        return carry

    lax.fori_loop(0, 2 * STEPS, exchange, 0)
    sent(2 * STEPS - 2)
    sent(2 * STEPS - 1)

    def finish(t, carry):
        arrived = received.at[0, pl.ds(0, 7), pl.ds(0, ROWS)]
        pltpu.make_async_copy(arrived, arrived, rec_sem.at[t]).wait()
        return carry

    lax.fori_loop(0, STEPS, finish, 0)

    def drain(micro, carry):
        eight, seven = obuf.at[micro], obuf.at[micro, pl.ds(0, 7)]

        @pl.when(odd == 0)
        def _():
            pltpu.make_async_copy(eight, eight, o_sem.at[micro]).wait()

        @pl.when(odd == 1)
        def _():
            pltpu.make_async_copy(seven, seven, p2_sem.at[micro, 0]).wait()

        @pl.when((odd == 1) & (s < last))
        def _():
            pltpu.make_async_copy(seven, seven, o_sem.at[micro]).wait()
            pltpu.make_async_copy(eight, eight, p2_sem.at[micro, 1]).wait()

        @pl.when(s == last)
        def _():
            others = fin_out.at[micro, pl.ds(0, last)]
            pltpu.make_async_copy(others, others, fin_send.at[micro]).wait()

        here = fin.at[micro]
        pltpu.make_async_copy(here, here, fin_sem.at[micro]).wait()
        finals[micro] = fin[micro]
        return carry

    lax.fori_loop(0, MICRO, drain, 0)


def relay_and_exchange(inputs, routes, partner, weights, momentum):
    bf16 = jnp.bfloat16
    dma = pltpu.SemaphoreType.DMA
    whole = pl.BlockSpec(memory_space=pltpu.VMEM)
    scalars = pl.BlockSpec(memory_space=pltpu.SMEM)
    anywhere = pl.BlockSpec(memory_space=pl.ANY)
    return pl.pallas_call(
        kernel,
        out_shape=(
            jax.ShapeDtypeStruct((MICRO, TOKENS, WIDTH // SECTIONS), bf16),
            jax.ShapeDtypeStruct((2, REPLICAS, SLICE, HIDDEN), bf16),
            jax.ShapeDtypeStruct((2, REPLICAS, SLICE, HIDDEN), bf16),
        ),
        in_specs=[anywhere, scalars, scalars, anywhere, anywhere],
        out_specs=(whole, anywhere, anywhere),
        scratch_shapes=[
            pltpu.VMEM((WIDTH, HIDDEN), bf16),
            pltpu.VMEM((HIDDEN, WIDTH), bf16),
            pltpu.VMEM((MICRO, REPLICAS, TOKENS, SLICE), bf16),
            pltpu.VMEM((MICRO, REPLICAS, TOKENS, SLICE), bf16),
            pltpu.VMEM((MICRO, 2, REPLICAS, TOKENS, SLICE), bf16),
            pltpu.VMEM((MICRO, 2, REPLICAS, TOKENS, SLICE), bf16),
            pltpu.VMEM((MICRO, TOKENS, WIDTH // SECTIONS), bf16),
            pltpu.VMEM((MICRO, SECTIONS, TOKENS, WIDTH // SECTIONS), bf16),
            pltpu.VMEM((REPLICAS, ROWS, HIDDEN), bf16),
            pltpu.VMEM((2, REPLICAS, ROWS, HIDDEN), bf16),
            dma,
            dma((MICRO, REPLICAS)),
            dma((MICRO,)),
            dma((MICRO, 2)),
            dma((MICRO, 2)),
            dma((MICRO,)),
            dma((MICRO,)),
            dma((STEPS,)),
            dma((2 * STEPS,)),
            dma((STEPS,)),
            dma((STEPS,)),
            dma,
        ],
        compiler_params=pltpu.CompilerParams(
            collective_id=1, has_side_effects=True, vmem_limit_bytes=48 * 2**20
        ),
        cost_estimate=pl.CostEstimate(
            flops=2**30, bytes_accessed=48 * 2**20, transcendentals=2**16
        ),
        name="relay_and_exchange",
    )(inputs, routes, partner, weights, momentum)


def body(inputs, routes, weights, anchor, momentum, partner):
    finals, _, received = relay_and_exchange(inputs[0], routes, partner, weights[0, 0], momentum[0, 0])
    shape = weights.shape
    others = received.reshape((2,) + shape)
    mean_weights = 0.5 * (weights.astype(jnp.float32) + others[0].astype(jnp.float32))
    mean_momentum = 0.5 * (momentum.astype(jnp.float32) + others[1].astype(jnp.float32))
    start_values = anchor.astype(jnp.float32)
    delta = start_values - mean_weights
    momentum_next = 0.9 * mean_momentum + delta
    new_weights = (start_values - 0.7 * (delta + 0.9 * momentum_next)).astype(jnp.bfloat16)
    return (finals[None], new_weights, momentum_next.astype(jnp.bfloat16))


def solution(mesh):
    in_specs = (
        P("replica", None, None, None),
        P(),
        P("replica", "section", None, None),
        P("replica", "section", None, None),
        P("replica", "section", None, None),
        P(),
    )
    out_specs = (
        P("replica", None, None, "section"),
        P("replica", "section", None, None),
        P("replica", "section", None, None),
    )
    return jax.shard_map(body, mesh=mesh, in_specs=in_specs, out_specs=out_specs, check_vma=False)
```

```python
import functools

import jax
import jax.numpy as jnp
from jax import lax
from jax.experimental import pallas as pl
from jax.experimental.pallas import tpu as pltpu
from jax.sharding import PartitionSpec as P

MESH = pl.DeviceIdType.MESH
FAR = (6, 2, 5, 7, 4, 1, 3)
NEAR = (0, 1, 3, 4, 5, 7, 2, 6)
REPLICAS = 8
SECTIONS = 16
MICRO = 4
TOKENS = 32
WIDTH = 4096
HIDDEN = 512
SLICE = WIDTH // REPLICAS
PIECES = 8
ROWS = SLICE // PIECES
STEPS = 2 * PIECES
TURNS = MICRO + 2
DEPTH = 3


def other_replica(r, k):
    x, y = lax.rem(r, 4), lax.div(r, 4)
    x = (x, x + 1 - 2 * lax.rem(x, 2), lax.rem(x + 2, 4), 3 - x)[k % 4]
    y = (y, 1 - y)[k // 4]
    return y * 4 + x


def before_relay(section):
    return 4 * lax.div(section, 2)


def beside_relay(odd):
    return 5, 5


def kernel(
    inputs, routes, partner, weights, momentum,
    finals, landed, received_w, received_m,
    wv, wt, xbuf, obuf, first, second, fin, fin_out, stage_in, stage_out,
    w_sem, x_sem, o_sem, p1_sem, p2_sem, fin_sem, fin_send, land_sem, bulk_send, rec_sem, own_sem, stage_sem, done_sem,
):
    r = lax.axis_index("replica")
    s = lax.axis_index("section")
    odd = lax.rem(s, 2)
    last = SECTIONS - 1

    load_w = pltpu.make_async_copy(weights, wv, w_sem)
    load_w.start()

    barrier = pltpu.get_barrier_semaphore()

    def greet(device):
        pl.semaphore_signal(barrier, inc=1, device_id=device, device_id_type=MESH)

    for k in range(1, 8):
        greet((other_replica(r, k), s))

    @pl.when(s > 0)
    def _():
        for k in range(8):
            greet((other_replica(r, k), s - 1))

    @pl.when(s < last - 1)
    def _():
        greet((r, last))

    @pl.when((odd == 0) & (s < last - 1))
    def _():
        greet((r, s + 1))

    pl.semaphore_wait(barrier, jnp.where(s < last, 15 + odd, 7 + last - 1))

    def slice_rows(q, piece):
        return pl.ds(pl.multiple_of(q * SLICE + piece * ROWS, ROWS), ROWS)

    def piece_rows(piece):
        return pl.ds(pl.multiple_of(piece * ROWS, ROWS), ROWS)

    def take_slices(step):
        array, piece = lax.div(step, PIECES), lax.rem(step, PIECES)
        for which, source in enumerate((weights, momentum)):

            @pl.when(array == which)
            def _():
                for k in FAR:
                    q = other_replica(r, k)
                    pltpu.make_async_remote_copy(
                        src_ref=source.at[slice_rows(q, piece)],
                        dst_ref=landed.at[which, r, piece_rows(piece)],
                        send_sem=bulk_send.at[step],
                        recv_sem=land_sem.at[step],
                        device_id=(q, s),
                        device_id_type=MESH,
                    ).start()
                pltpu.make_async_copy(
                    source.at[slice_rows(r, piece)],
                    landed.at[which, r, piece_rows(piece)],
                    land_sem.at[step],
                ).start()

    def pass_on(step):
        array, piece = lax.div(step, PIECES), lax.rem(step, PIECES)
        slot = lax.rem(step, DEPTH)
        arrived = landed.at[array, :, piece_rows(piece)]
        pltpu.make_async_copy(arrived, arrived, land_sem.at[step]).wait()
        fetch = pltpu.make_async_copy(arrived, stage_in, stage_sem)
        fetch.start()
        fetch.wait()
        for k in FAR + (0,):
            d = other_replica(r, k)
            stage_out[slot, d] = stage_in[partner[d]]
        for which, received in enumerate((received_w, received_m)):

            @pl.when(array == which)
            def _():
                for k in FAR:
                    d = other_replica(r, k)
                    pltpu.make_async_remote_copy(
                        src_ref=stage_out.at[slot, d],
                        dst_ref=received.at[r, piece_rows(piece)],
                        send_sem=bulk_send.at[STEPS + step],
                        recv_sem=rec_sem.at[step],
                        device_id=(d, s),
                        device_id_type=MESH,
                    ).start()
                pltpu.make_async_copy(
                    stage_out.at[slot, r],
                    received.at[r, piece_rows(piece)],
                    own_sem.at[step],
                ).start()

    def sent(step):
        some = landed.at[0, pl.ds(0, 7), pl.ds(0, ROWS)]
        pltpu.make_async_copy(some, some, bulk_send.at[step]).wait()

        @pl.when(step >= STEPS)
        def _():
            one = stage_out.at[0, 0]
            pltpu.make_async_copy(one, one, own_sem.at[step - STEPS]).wait()

    def route(micro, way):
        whole = first.at[micro, way]
        pltpu.make_async_copy(whole, whole, p1_sem.at[micro, way]).wait()
        row = s - 1 + way
        targets = [routes[micro, row, source] for source in range(REPLICAS)]
        for k in FAR + (0,):
            d = other_replica(r, k)
            chosen = first[micro, way, 0]
            for source in range(1, REPLICAS):
                chosen = jnp.where(targets[source] == d, first[micro, way, source], chosen)
            second[micro, way, d] = chosen
            passing = functools.partial(
                pltpu.make_async_remote_copy,
                src_ref=second.at[micro, way, d],
                dst_ref=xbuf.at[micro, r],
                send_sem=p2_sem.at[micro, way],
                recv_sem=x_sem.at[micro, r],
                device_id=(d, s + way),
                device_id_type=MESH,
            )
            if k or way:
                passing().start()
            else:
                pltpu.make_async_copy(second.at[micro, way, d], xbuf.at[micro, r], x_sem.at[micro, r]).start()

    def apply_section(micro):
        before = jnp.zeros((TOKENS, HIDDEN), jnp.float32)
        squares = jnp.zeros((TOKENS, 128), jnp.float32)
        for k in NEAR:
            q = other_replica(r, k)
            here = xbuf.at[micro, q]
            pltpu.make_async_copy(here, here, x_sem.at[micro, q]).wait()
            block = xbuf[micro, q]
            rows = pl.ds(pl.multiple_of(q * SLICE, SLICE), SLICE)
            before = before + jnp.dot(block, wv[rows, :], preferred_element_type=jnp.float32)
            values = block.astype(jnp.float32)
            values = values * values
            for c in range(SLICE // 128):
                squares = squares + values[:, c * 128 : (c + 1) * 128]
        factor = lax.rsqrt(jnp.sum(squares, axis=-1, keepdims=True) * (1.0 / WIDTH) + 1e-05)
        before = before * (factor * WIDTH ** (-0.5))
        hidden = jax.nn.silu(before).astype(jnp.bfloat16)

        def leaving(q):
            columns = pl.ds(pl.multiple_of(q * SLICE, SLICE), SLICE)
            branch = jnp.dot(hidden, wt[:, columns], preferred_element_type=jnp.float32)
            return (xbuf[micro, q].astype(jnp.float32) + branch * HIDDEN ** (-0.5)).astype(jnp.bfloat16)

        @pl.when(s < last)
        def _():
            for k in FAR + (0,):
                q = other_replica(r, k)
                obuf[micro, q] = leaving(q)
                remote = pltpu.make_async_remote_copy(
                    src_ref=obuf.at[micro, q],
                    dst_ref=first.at[micro, odd, r],
                    send_sem=o_sem.at[micro],
                    recv_sem=p1_sem.at[micro, odd],
                    device_id=(q, s + 1 - odd),
                    device_id_type=MESH,
                )
                if k:
                    remote.start()
                else:
                    pl.when(odd == 0)(remote.start)

                    @pl.when(odd == 1)
                    def _():
                        pltpu.make_async_copy(
                            obuf.at[micro, q], first.at[micro, 1, r], p1_sem.at[micro, 1]
                        ).start()

        @pl.when(s == last)
        def _():
            half = SLICE // 2
            for q in range(REPLICAS):
                block = leaving(q)
                for side in range(2):
                    section = 2 * q + side
                    fin_out[micro, section] = block[:, side * half : (side + 1) * half]
                    if section < last:
                        pltpu.make_async_remote_copy(
                            src_ref=fin_out.at[micro, section],
                            dst_ref=fin.at[micro],
                            send_sem=fin_send.at[micro],
                            recv_sem=fin_sem.at[micro],
                            device_id=(r, section),
                            device_id_type=MESH,
                        ).start()
                    else:
                        pltpu.make_async_copy(
                            fin_out.at[micro, section], fin.at[micro], fin_sem.at[micro]
                        ).start()

    def relay_turn(t):
        @pl.when((odd == 1) & (s < last) & (t >= 2))
        def _():
            route(t - 2, 1)

        @pl.when((t >= 1) & (t < MICRO + 1))
        def _():
            apply_section(t - 1)

        @pl.when((odd == 1) & (t < MICRO))
        def _():
            route(t, 0)

        @pl.when((odd == 1) & (s < last) & (t == TURNS - 1))
        def _():
            pl.semaphore_signal(done_sem, inc=1, device_id=(r, s - 1), device_id_type=MESH)

        @pl.when((odd == 0) & (s < last - 1) & (t == TURNS - 1))
        def _():
            pl.semaphore_wait(done_sem, 1)

    @pl.when(s == 0)
    def _():
        for micro in range(MICRO):
            for q in range(REPLICAS):
                pltpu.make_async_copy(
                    inputs.at[micro, :, pl.ds(q * SLICE, SLICE)], xbuf.at[micro, q], x_sem.at[micro, q]
                ).start()

    ahead = before_relay(s)
    fill_first, fill_end = beside_relay(odd)

    def advance(u, carry):
        turn = u - ahead

        @pl.when(u == jnp.maximum(ahead - 1, 0))
        def _():
            load_w.wait()
            wt[...] = wv[...].T

        @pl.when((turn >= 0) & (turn < TURNS))
        def _():
            relay_turn(turn)

        beside = (turn >= fill_first) & (turn < fill_end)
        step = jnp.where(turn < 0, u, jnp.where(turn < TURNS, u - fill_first, u - TURNS + fill_end - fill_first))
        due = ((turn < 0) | (turn >= TURNS) | beside) & (step < 2 * STEPS)

        @pl.when(due & (step >= DEPTH))
        def _():
            sent(step - DEPTH)

        @pl.when(due & (step < STEPS))
        def _():
            take_slices(step)

        @pl.when(due & (step >= STEPS))
        def _():
            pass_on(step - STEPS)

        return carry

    lax.fori_loop(0, 2 * STEPS + TURNS, advance, 0)
    for step in range(2 * STEPS - DEPTH, 2 * STEPS):
        sent(step)

    def finish(t, carry):
        arrived = received_w.at[pl.ds(0, 7), pl.ds(0, ROWS)]
        pltpu.make_async_copy(arrived, arrived, rec_sem.at[t]).wait()
        return carry

    lax.fori_loop(0, STEPS, finish, 0)

    def drain(micro, carry):
        eight, seven = obuf.at[micro], obuf.at[micro, pl.ds(0, 7)]

        @pl.when(odd == 0)
        def _():
            pltpu.make_async_copy(eight, eight, o_sem.at[micro]).wait()

        @pl.when(odd == 1)
        def _():
            pltpu.make_async_copy(seven, seven, p2_sem.at[micro, 0]).wait()

        @pl.when((odd == 1) & (s < last))
        def _():
            pltpu.make_async_copy(seven, seven, o_sem.at[micro]).wait()
            pltpu.make_async_copy(eight, eight, p2_sem.at[micro, 1]).wait()

        @pl.when(s == last)
        def _():
            others = fin_out.at[micro, pl.ds(0, last)]
            pltpu.make_async_copy(others, others, fin_send.at[micro]).wait()

        here = fin.at[micro]
        pltpu.make_async_copy(here, here, fin_sem.at[micro]).wait()
        finals[micro] = fin[micro]
        return carry

    lax.fori_loop(0, MICRO, drain, 0)


def relay_and_exchange(inputs, routes, partner, weights, momentum):
    bf16 = jnp.bfloat16
    dma = pltpu.SemaphoreType.DMA
    whole = pl.BlockSpec(memory_space=pltpu.VMEM)
    scalars = pl.BlockSpec(memory_space=pltpu.SMEM)
    anywhere = pl.BlockSpec(memory_space=pl.ANY)
    return pl.pallas_call(
        kernel,
        out_shape=(
            jax.ShapeDtypeStruct((MICRO, TOKENS, WIDTH // SECTIONS), bf16),
            jax.ShapeDtypeStruct((2, REPLICAS, SLICE, HIDDEN), bf16),
            jax.ShapeDtypeStruct((REPLICAS, SLICE, HIDDEN), bf16),
            jax.ShapeDtypeStruct((REPLICAS, SLICE, HIDDEN), bf16),
        ),
        in_specs=[anywhere, scalars, scalars, anywhere, anywhere],
        out_specs=(whole, anywhere, anywhere, anywhere),
        scratch_shapes=[
            pltpu.VMEM((WIDTH, HIDDEN), bf16),
            pltpu.VMEM((HIDDEN, WIDTH), bf16),
            pltpu.VMEM((MICRO, REPLICAS, TOKENS, SLICE), bf16),
            pltpu.VMEM((MICRO, REPLICAS, TOKENS, SLICE), bf16),
            pltpu.VMEM((MICRO, 2, REPLICAS, TOKENS, SLICE), bf16),
            pltpu.VMEM((MICRO, 2, REPLICAS, TOKENS, SLICE), bf16),
            pltpu.VMEM((MICRO, TOKENS, WIDTH // SECTIONS), bf16),
            pltpu.VMEM((MICRO, SECTIONS, TOKENS, WIDTH // SECTIONS), bf16),
            pltpu.VMEM((REPLICAS, ROWS, HIDDEN), bf16),
            pltpu.VMEM((DEPTH, REPLICAS, ROWS, HIDDEN), bf16),
            dma,
            dma((MICRO, REPLICAS)),
            dma((MICRO,)),
            dma((MICRO, 2)),
            dma((MICRO, 2)),
            dma((MICRO,)),
            dma((MICRO,)),
            dma((STEPS,)),
            dma((2 * STEPS,)),
            dma((STEPS,)),
            dma((STEPS,)),
            dma,
            pltpu.SemaphoreType.REGULAR,
        ],
        compiler_params=pltpu.CompilerParams(
            collective_id=1, has_side_effects=True, vmem_limit_bytes=48 * 2**20
        ),
        cost_estimate=pl.CostEstimate(
            flops=2**30, bytes_accessed=48 * 2**20, transcendentals=2**16
        ),
        name="relay_and_exchange",
    )(inputs, routes, partner, weights, momentum)


def body(inputs, routes, weights, anchor, momentum, partner):
    finals, _, other_weights, other_momentum = relay_and_exchange(inputs[0], routes, partner, weights[0, 0], momentum[0, 0])
    shape = weights.shape
    mean_weights = 0.5 * (weights.astype(jnp.float32) + other_weights.reshape(shape).astype(jnp.float32))
    mean_momentum = 0.5 * (momentum.astype(jnp.float32) + other_momentum.reshape(shape).astype(jnp.float32))
    start_values = anchor.astype(jnp.float32)
    delta = start_values - mean_weights
    momentum_next = 0.9 * mean_momentum + delta
    new_weights = (start_values - 0.7 * (delta + 0.9 * momentum_next)).astype(jnp.bfloat16)
    return (finals[None], new_weights, momentum_next.astype(jnp.bfloat16))


def solution(mesh):
    in_specs = (
        P("replica", None, None, None),
        P(),
        P("replica", "section", None, None),
        P("replica", "section", None, None),
        P("replica", "section", None, None),
        P(),
    )
    out_specs = (
        P("replica", None, None, "section"),
        P("replica", "section", None, None),
        P("replica", "section", None, None),
    )
    return jax.shard_map(body, mesh=mesh, in_specs=in_specs, out_specs=out_specs, check_vma=False)
```

```python
import functools

import jax
import jax.numpy as jnp
from jax import lax
from jax.experimental import pallas as pl
from jax.experimental.pallas import tpu as pltpu
from jax.sharding import PartitionSpec as P

MESH = pl.DeviceIdType.MESH
FAR = (6, 2, 5, 7, 4, 1, 3)
NEAR = (0, 1, 3, 4, 5, 7, 2, 6)
REPLICAS = 8
SECTIONS = 16
MICRO = 4
TOKENS = 32
WIDTH = 4096
HIDDEN = 512
SLICE = WIDTH // REPLICAS
PIECES = 8
ROWS = SLICE // PIECES
STEPS = 2 * PIECES
TURNS = MICRO + 2
DEPTH = 3


def other_replica(r, k):
    x, y = lax.rem(r, 4), lax.div(r, 4)
    x = (x, x + 1 - 2 * lax.rem(x, 2), lax.rem(x + 2, 4), 3 - x)[k % 4]
    y = (y, 1 - y)[k // 4]
    return y * 4 + x


def before_relay(section):
    return 1 + 4 * lax.div(section, 2) + jnp.minimum(lax.div(section, 2), 1) + lax.div(section, 8)


def beside_relay(odd):
    return 5, 5


def kernel(
    inputs, routes, partner, weights, momentum,
    finals, landed, received_w, received_m,
    wv, wt, xbuf, obuf, first, second, fin, fin_out, stage_in, stage_out,
    w_sem, x_sem, o_sem, p1_sem, p2_sem, fin_sem, fin_send, land_sem, bulk_send, rec_sem, own_sem, stage_sem, done_sem,
):
    r = lax.axis_index("replica")
    s = lax.axis_index("section")
    odd = lax.rem(s, 2)
    last = SECTIONS - 1

    load_w = pltpu.make_async_copy(weights, wv, w_sem)
    load_w.start()

    barrier = pltpu.get_barrier_semaphore()

    def greet(device):
        pl.semaphore_signal(barrier, inc=1, device_id=device, device_id_type=MESH)

    for k in range(1, 8):
        greet((other_replica(r, k), s))

    @pl.when(s > 0)
    def _():
        for k in range(8):
            greet((other_replica(r, k), s - 1))

    @pl.when(s < last - 1)
    def _():
        greet((r, last))

    @pl.when((odd == 0) & (s < last - 1))
    def _():
        greet((r, s + 1))

    pl.semaphore_wait(barrier, jnp.where(s < last, 15 + odd, 7 + last - 1))

    def slice_rows(q, piece):
        return pl.ds(pl.multiple_of(q * SLICE + piece * ROWS, ROWS), ROWS)

    def piece_rows(piece):
        return pl.ds(pl.multiple_of(piece * ROWS, ROWS), ROWS)

    def take_slices(step):
        array, piece = lax.div(step, PIECES), lax.rem(step, PIECES)
        for which, source in enumerate((weights, momentum)):

            @pl.when(array == which)
            def _():
                for k in FAR:
                    q = other_replica(r, k)
                    pltpu.make_async_remote_copy(
                        src_ref=source.at[slice_rows(q, piece)],
                        dst_ref=landed.at[which, r, piece_rows(piece)],
                        send_sem=bulk_send.at[step],
                        recv_sem=land_sem.at[step],
                        device_id=(q, s),
                        device_id_type=MESH,
                    ).start()
                pltpu.make_async_copy(
                    source.at[slice_rows(r, piece)],
                    landed.at[which, r, piece_rows(piece)],
                    land_sem.at[step],
                ).start()

    def pass_on(step):
        array, piece = lax.div(step, PIECES), lax.rem(step, PIECES)
        slot = lax.rem(step, DEPTH)
        arrived = landed.at[array, :, piece_rows(piece)]
        pltpu.make_async_copy(arrived, arrived, land_sem.at[step]).wait()
        fetch = pltpu.make_async_copy(arrived, stage_in, stage_sem)
        fetch.start()
        fetch.wait()
        for k in FAR + (0,):
            d = other_replica(r, k)
            stage_out[slot, d] = stage_in[partner[d]]
        for which, received in enumerate((received_w, received_m)):

            @pl.when(array == which)
            def _():
                for k in FAR:
                    d = other_replica(r, k)
                    pltpu.make_async_remote_copy(
                        src_ref=stage_out.at[slot, d],
                        dst_ref=received.at[r, piece_rows(piece)],
                        send_sem=bulk_send.at[STEPS + step],
                        recv_sem=rec_sem.at[step],
                        device_id=(d, s),
                        device_id_type=MESH,
                    ).start()
                pltpu.make_async_copy(
                    stage_out.at[slot, r],
                    received.at[r, piece_rows(piece)],
                    own_sem.at[step],
                ).start()

    def sent(step):
        some = landed.at[0, pl.ds(0, 7), pl.ds(0, ROWS)]
        pltpu.make_async_copy(some, some, bulk_send.at[step]).wait()

        @pl.when(step >= STEPS)
        def _():
            one = stage_out.at[0, 0]
            pltpu.make_async_copy(one, one, own_sem.at[step - STEPS]).wait()

    def route(micro, way):
        whole = first.at[micro, way]
        pltpu.make_async_copy(whole, whole, p1_sem.at[micro, way]).wait()
        row = s - 1 + way
        targets = [routes[micro, source, row] for source in range(REPLICAS)]
        for k in FAR + (0,):
            d = other_replica(r, k)
            chosen = first[micro, way, 0]
            for source in range(1, REPLICAS):
                chosen = jnp.where(targets[source] == d, first[micro, way, source], chosen)
            second[micro, way, d] = chosen
            passing = functools.partial(
                pltpu.make_async_remote_copy,
                src_ref=second.at[micro, way, d],
                dst_ref=xbuf.at[micro, r],
                send_sem=p2_sem.at[micro, way],
                recv_sem=x_sem.at[micro, r],
                device_id=(d, s + way),
                device_id_type=MESH,
            )
            if k or way:
                passing().start()
            else:
                pltpu.make_async_copy(second.at[micro, way, d], xbuf.at[micro, r], x_sem.at[micro, r]).start()

    def apply_section(micro):
        before = jnp.zeros((TOKENS, HIDDEN), jnp.float32)
        squares = jnp.zeros((TOKENS, 128), jnp.float32)
        for k in NEAR:
            q = other_replica(r, k)
            here = xbuf.at[micro, q]
            pltpu.make_async_copy(here, here, x_sem.at[micro, q]).wait()
            block = xbuf[micro, q]
            rows = pl.ds(pl.multiple_of(q * SLICE, SLICE), SLICE)
            before = before + jnp.dot(block, wv[rows, :], preferred_element_type=jnp.float32)
            values = block.astype(jnp.float32)
            values = values * values
            for c in range(SLICE // 128):
                squares = squares + values[:, c * 128 : (c + 1) * 128]
        factor = lax.rsqrt(jnp.sum(squares, axis=-1, keepdims=True) * (1.0 / WIDTH) + 1e-05)
        before = before * (factor * WIDTH ** (-0.5))
        hidden = jax.nn.silu(before).astype(jnp.bfloat16)

        def leaving(q):
            columns = pl.ds(pl.multiple_of(q * SLICE, SLICE), SLICE)
            branch = jnp.dot(hidden, wt[:, columns], preferred_element_type=jnp.float32)
            return (xbuf[micro, q].astype(jnp.float32) + branch * HIDDEN ** (-0.5)).astype(jnp.bfloat16)

        @pl.when(s < last)
        def _():
            for k in FAR + (0,):
                q = other_replica(r, k)
                obuf[micro, q] = leaving(q)
                remote = pltpu.make_async_remote_copy(
                    src_ref=obuf.at[micro, q],
                    dst_ref=first.at[micro, odd, r],
                    send_sem=o_sem.at[micro],
                    recv_sem=p1_sem.at[micro, odd],
                    device_id=(q, s + 1 - odd),
                    device_id_type=MESH,
                )
                if k:
                    remote.start()
                else:
                    pl.when(odd == 0)(remote.start)

                    @pl.when(odd == 1)
                    def _():
                        pltpu.make_async_copy(
                            obuf.at[micro, q], first.at[micro, 1, r], p1_sem.at[micro, 1]
                        ).start()

        @pl.when(s == last)
        def _():
            half = SLICE // 2
            for q in range(REPLICAS):
                block = leaving(q)
                for side in range(2):
                    section = 2 * q + side
                    fin_out[micro, section] = block[:, side * half : (side + 1) * half]
                    if section < last:
                        pltpu.make_async_remote_copy(
                            src_ref=fin_out.at[micro, section],
                            dst_ref=fin.at[micro],
                            send_sem=fin_send.at[micro],
                            recv_sem=fin_sem.at[micro],
                            device_id=(r, section),
                            device_id_type=MESH,
                        ).start()
                    else:
                        pltpu.make_async_copy(
                            fin_out.at[micro, section], fin.at[micro], fin_sem.at[micro]
                        ).start()

    def relay_turn(t):
        @pl.when((odd == 1) & (t < MICRO))
        def _():
            route(t, 0)

        @pl.when((t >= 1) & (t < MICRO + 1))
        def _():
            apply_section(t - 1)

        @pl.when((odd == 1) & (s < last) & (t >= 2))
        def _():
            route(t - 2, 1)

        @pl.when((odd == 1) & (s < last) & (t == TURNS - 1))
        def _():
            pl.semaphore_signal(done_sem, inc=1, device_id=(r, s - 1), device_id_type=MESH)

        @pl.when((odd == 0) & (s < last - 1) & (t == TURNS - 1))
        def _():
            pl.semaphore_wait(done_sem, 1)

    @pl.when(s == 0)
    def _():
        for micro in range(MICRO):
            for q in range(REPLICAS):
                pltpu.make_async_copy(
                    inputs.at[micro, :, pl.ds(q * SLICE, SLICE)], xbuf.at[micro, q], x_sem.at[micro, q]
                ).start()

    ahead = before_relay(s)
    fill_first, fill_end = beside_relay(odd)

    def advance(u, carry):
        turn = u - ahead

        @pl.when(u == jnp.maximum(ahead - 1, 0))
        def _():
            load_w.wait()
            wt[...] = wv[...].T

        @pl.when((turn >= 0) & (turn < TURNS))
        def _():
            relay_turn(turn)

        beside = (turn >= fill_first) & (turn < fill_end)
        step = jnp.where(turn < 0, u, jnp.where(turn < TURNS, u - fill_first, u - TURNS + fill_end - fill_first))
        due = ((turn < 0) | (turn >= TURNS) | beside) & (step < 2 * STEPS)

        @pl.when(due & (step >= DEPTH))
        def _():
            sent(step - DEPTH)

        @pl.when(due & (step < STEPS))
        def _():
            take_slices(step)

        @pl.when(due & (step >= STEPS))
        def _():
            pass_on(step - STEPS)

        return carry

    lax.fori_loop(0, 2 * STEPS + TURNS, advance, 0)
    for step in range(2 * STEPS - DEPTH, 2 * STEPS):
        sent(step)

    def finish(t, carry):
        arrived = received_w.at[pl.ds(0, 7), pl.ds(0, ROWS)]
        pltpu.make_async_copy(arrived, arrived, rec_sem.at[t]).wait()
        return carry

    lax.fori_loop(0, STEPS, finish, 0)

    def drain(micro, carry):
        eight, seven = obuf.at[micro], obuf.at[micro, pl.ds(0, 7)]

        @pl.when(odd == 0)
        def _():
            pltpu.make_async_copy(eight, eight, o_sem.at[micro]).wait()

        @pl.when(odd == 1)
        def _():
            pltpu.make_async_copy(seven, seven, p2_sem.at[micro, 0]).wait()

        @pl.when((odd == 1) & (s < last))
        def _():
            pltpu.make_async_copy(seven, seven, o_sem.at[micro]).wait()
            pltpu.make_async_copy(eight, eight, p2_sem.at[micro, 1]).wait()

        @pl.when(s == last)
        def _():
            others = fin_out.at[micro, pl.ds(0, last)]
            pltpu.make_async_copy(others, others, fin_send.at[micro]).wait()

        here = fin.at[micro]
        pltpu.make_async_copy(here, here, fin_sem.at[micro]).wait()
        finals[micro] = fin[micro]
        return carry

    lax.fori_loop(0, MICRO, drain, 0)


def relay_and_exchange(inputs, routes, partner, weights, momentum):
    bf16 = jnp.bfloat16
    dma = pltpu.SemaphoreType.DMA
    whole = pl.BlockSpec(memory_space=pltpu.VMEM)
    scalars = pl.BlockSpec(memory_space=pltpu.SMEM)
    anywhere = pl.BlockSpec(memory_space=pl.ANY)
    far_off = pl.BlockSpec(memory_space=pltpu.HBM)
    return pl.pallas_call(
        kernel,
        out_shape=(
            jax.ShapeDtypeStruct((MICRO, TOKENS, WIDTH // SECTIONS), bf16),
            jax.ShapeDtypeStruct((2, REPLICAS, SLICE, HIDDEN), bf16),
            jax.ShapeDtypeStruct((REPLICAS, SLICE, HIDDEN), bf16),
            jax.ShapeDtypeStruct((REPLICAS, SLICE, HIDDEN), bf16),
        ),
        in_specs=[far_off, scalars, scalars, far_off, far_off],
        out_specs=(whole, anywhere, anywhere, anywhere),
        scratch_shapes=[
            pltpu.VMEM((WIDTH, HIDDEN), bf16),
            pltpu.VMEM((HIDDEN, WIDTH), bf16),
            pltpu.VMEM((MICRO, REPLICAS, TOKENS, SLICE), bf16),
            pltpu.VMEM((MICRO, REPLICAS, TOKENS, SLICE), bf16),
            pltpu.VMEM((MICRO, 2, REPLICAS, TOKENS, SLICE), bf16),
            pltpu.VMEM((MICRO, 2, REPLICAS, TOKENS, SLICE), bf16),
            pltpu.VMEM((MICRO, TOKENS, WIDTH // SECTIONS), bf16),
            pltpu.VMEM((MICRO, SECTIONS, TOKENS, WIDTH // SECTIONS), bf16),
            pltpu.VMEM((REPLICAS, ROWS, HIDDEN), bf16),
            pltpu.VMEM((DEPTH, REPLICAS, ROWS, HIDDEN), bf16),
            dma,
            dma((MICRO, REPLICAS)),
            dma((MICRO,)),
            dma((MICRO, 2)),
            dma((MICRO, 2)),
            dma((MICRO,)),
            dma((MICRO,)),
            dma((STEPS,)),
            dma((2 * STEPS,)),
            dma((STEPS,)),
            dma((STEPS,)),
            dma,
            pltpu.SemaphoreType.REGULAR,
        ],
        compiler_params=pltpu.CompilerParams(
            collective_id=1, has_side_effects=True, vmem_limit_bytes=48 * 2**20
        ),
        cost_estimate=pl.CostEstimate(
            flops=2**30, bytes_accessed=48 * 2**20, transcendentals=2**16
        ),
        name="relay_and_exchange",
    )(inputs, routes, partner, weights, momentum)


def body(inputs, routes, weights, anchor, momentum, partner):
    finals, _, other_weights, other_momentum = relay_and_exchange(inputs[0], jnp.swapaxes(routes, 1, 2), partner, weights[0, 0], momentum[0, 0])
    shape = weights.shape
    mean_weights = 0.5 * (weights.astype(jnp.float32) + other_weights.reshape(shape).astype(jnp.float32))
    mean_momentum = 0.5 * (momentum.astype(jnp.float32) + other_momentum.reshape(shape).astype(jnp.float32))
    start_values = anchor.astype(jnp.float32)
    delta = start_values - mean_weights
    momentum_next = 0.9 * mean_momentum + delta
    new_weights = (start_values - 0.7 * (delta + 0.9 * momentum_next)).astype(jnp.bfloat16)
    return (finals[None], new_weights, momentum_next.astype(jnp.bfloat16))


def solution(mesh):
    in_specs = (
        P("replica", None, None, None),
        P(),
        P("replica", "section", None, None),
        P("replica", "section", None, None),
        P("replica", "section", None, None),
        P(),
    )
    out_specs = (
        P("replica", None, None, "section"),
        P("replica", "section", None, None),
        P("replica", "section", None, None),
    )
    return jax.shard_map(body, mesh=mesh, in_specs=in_specs, out_specs=out_specs, check_vma=False)
```

```python
import functools

import jax
import jax.numpy as jnp
from jax import lax
from jax.experimental import pallas as pl
from jax.experimental.pallas import tpu as pltpu
from jax.sharding import PartitionSpec as P

MESH = pl.DeviceIdType.MESH
FAR = (6, 2, 5, 7, 4, 1, 3)
NEAR = (0, 1, 3, 4, 5, 7, 2, 6)
REPLICAS = 8
SECTIONS = 16
MICRO = 4
TOKENS = 32
WIDTH = 4096
HIDDEN = 512
SLICE = WIDTH // REPLICAS
PIECES = 8
ROWS = SLICE // PIECES
STEPS = 2 * PIECES
TURNS = MICRO + 2
DEPTH = 3


def other_replica(r, k):
    x, y = lax.rem(r, 4), lax.div(r, 4)
    x = (x, x + 1 - 2 * lax.rem(x, 2), lax.rem(x + 2, 4), 3 - x)[k % 4]
    y = (y, 1 - y)[k // 4]
    return y * 4 + x


def before_relay(section):
    return 1 + 4 * lax.div(section, 2) + jnp.minimum(lax.div(section, 2), 1) + lax.div(section, 8)


def beside_relay(odd):
    return 5, 5


def kernel(
    inputs, routes, partner, weights, momentum, anchor,
    finals, landed, received_w, received_m, new_w, new_m,
    wv, near_m, near_a, got, wt, xbuf, obuf, first, second, fin, fin_out, stage_in, stage_out,
    w_sem, x_sem, o_sem, p1_sem, p2_sem, fin_sem, fin_send, land_sem, bulk_send, rec_sem, own_sem, stage_sem, done_sem, m_sem, a_sem, got_sem,
):
    r = lax.axis_index("replica")
    s = lax.axis_index("section")
    odd = lax.rem(s, 2)
    last = SECTIONS - 1

    load_w = pltpu.make_async_copy(weights, wv, w_sem)
    load_w.start()
    load_m = pltpu.make_async_copy(momentum, near_m, m_sem)
    load_a = pltpu.make_async_copy(anchor, near_a, a_sem)

    barrier = pltpu.get_barrier_semaphore()

    def greet(device):
        pl.semaphore_signal(barrier, inc=1, device_id=device, device_id_type=MESH)

    for k in range(1, 8):
        greet((other_replica(r, k), s))

    @pl.when(s > 0)
    def _():
        for k in range(8):
            greet((other_replica(r, k), s - 1))

    @pl.when(s < last - 1)
    def _():
        greet((r, last))

    @pl.when((odd == 0) & (s < last - 1))
    def _():
        greet((r, s + 1))

    pl.semaphore_wait(barrier, jnp.where(s < last, 15 + odd, 7 + last - 1))

    def slice_rows(q, piece):
        return pl.ds(pl.multiple_of(q * SLICE + piece * ROWS, ROWS), ROWS)

    def piece_rows(piece):
        return pl.ds(pl.multiple_of(piece * ROWS, ROWS), ROWS)

    def take_slices(step):
        array, piece = lax.rem(step, 2), lax.div(step, 2)
        for which, source in enumerate((weights, momentum)):

            @pl.when(array == which)
            def _():
                for k in FAR:
                    q = other_replica(r, k)
                    pltpu.make_async_remote_copy(
                        src_ref=source.at[slice_rows(q, piece)],
                        dst_ref=landed.at[which, r, piece_rows(piece)],
                        send_sem=bulk_send.at[step],
                        recv_sem=land_sem.at[step],
                        device_id=(q, s),
                        device_id_type=MESH,
                    ).start()
                pltpu.make_async_copy(
                    source.at[slice_rows(r, piece)],
                    landed.at[which, r, piece_rows(piece)],
                    land_sem.at[step],
                ).start()

    def pass_on(step):
        array, piece = lax.rem(step, 2), lax.div(step, 2)
        slot = lax.rem(step, DEPTH)
        arrived = landed.at[array, :, piece_rows(piece)]
        pltpu.make_async_copy(arrived, arrived, land_sem.at[step]).wait()
        fetch = pltpu.make_async_copy(arrived, stage_in, stage_sem)
        fetch.start()
        fetch.wait()
        for k in FAR + (0,):
            d = other_replica(r, k)
            stage_out[slot, d] = stage_in[partner[d]]
        for which, received in enumerate((received_w, received_m)):

            @pl.when(array == which)
            def _():
                for k in FAR:
                    d = other_replica(r, k)
                    pltpu.make_async_remote_copy(
                        src_ref=stage_out.at[slot, d],
                        dst_ref=received.at[r, piece_rows(piece)],
                        send_sem=bulk_send.at[STEPS + step],
                        recv_sem=rec_sem.at[step],
                        device_id=(d, s),
                        device_id_type=MESH,
                    ).start()
                pltpu.make_async_copy(
                    stage_out.at[slot, r],
                    received.at[r, piece_rows(piece)],
                    own_sem.at[step],
                ).start()

    def sent(step):
        some = landed.at[0, pl.ds(0, 7), pl.ds(0, ROWS)]
        pltpu.make_async_copy(some, some, bulk_send.at[step]).wait()

        @pl.when(step >= STEPS)
        def _():
            one = stage_out.at[0, 0]
            pltpu.make_async_copy(one, one, own_sem.at[step - STEPS]).wait()

    def route(micro, way):
        whole = first.at[micro, way]
        pltpu.make_async_copy(whole, whole, p1_sem.at[micro, way]).wait()
        row = s - 1 + way
        targets = [routes[micro, source, row] for source in range(REPLICAS)]
        for k in FAR + (0,):
            d = other_replica(r, k)
            chosen = first[micro, way, 0]
            for source in range(1, REPLICAS):
                chosen = jnp.where(targets[source] == d, first[micro, way, source], chosen)
            second[micro, way, d] = chosen
            passing = functools.partial(
                pltpu.make_async_remote_copy,
                src_ref=second.at[micro, way, d],
                dst_ref=xbuf.at[micro, r],
                send_sem=p2_sem.at[micro, way],
                recv_sem=x_sem.at[micro, r],
                device_id=(d, s + way),
                device_id_type=MESH,
            )
            if k or way:
                passing().start()
            else:
                pltpu.make_async_copy(second.at[micro, way, d], xbuf.at[micro, r], x_sem.at[micro, r]).start()

    def apply_section(micro):
        before = jnp.zeros((TOKENS, HIDDEN), jnp.float32)
        squares = jnp.zeros((TOKENS, 128), jnp.float32)
        for k in NEAR:
            q = other_replica(r, k)
            here = xbuf.at[micro, q]
            pltpu.make_async_copy(here, here, x_sem.at[micro, q]).wait()
            block = xbuf[micro, q]
            rows = pl.ds(pl.multiple_of(q * SLICE, SLICE), SLICE)
            before = before + jnp.dot(block, wv[rows, :], preferred_element_type=jnp.float32)
            values = block.astype(jnp.float32)
            values = values * values
            for c in range(SLICE // 128):
                squares = squares + values[:, c * 128 : (c + 1) * 128]
        factor = lax.rsqrt(jnp.sum(squares, axis=-1, keepdims=True) * (1.0 / WIDTH) + 1e-05)
        before = before * (factor * WIDTH ** (-0.5))
        hidden = jax.nn.silu(before).astype(jnp.bfloat16)

        def leaving(q):
            columns = pl.ds(pl.multiple_of(q * SLICE, SLICE), SLICE)
            branch = jnp.dot(hidden, wt[:, columns], preferred_element_type=jnp.float32)
            return (xbuf[micro, q].astype(jnp.float32) + branch * HIDDEN ** (-0.5)).astype(jnp.bfloat16)

        @pl.when(s < last)
        def _():
            for k in FAR + (0,):
                q = other_replica(r, k)
                obuf[micro, q] = leaving(q)
                remote = pltpu.make_async_remote_copy(
                    src_ref=obuf.at[micro, q],
                    dst_ref=first.at[micro, odd, r],
                    send_sem=o_sem.at[micro],
                    recv_sem=p1_sem.at[micro, odd],
                    device_id=(q, s + 1 - odd),
                    device_id_type=MESH,
                )
                if k:
                    remote.start()
                else:
                    pl.when(odd == 0)(remote.start)

                    @pl.when(odd == 1)
                    def _():
                        pltpu.make_async_copy(
                            obuf.at[micro, q], first.at[micro, 1, r], p1_sem.at[micro, 1]
                        ).start()

        @pl.when(s == last)
        def _():
            half = SLICE // 2
            for q in range(REPLICAS):
                block = leaving(q)
                for side in range(2):
                    section = 2 * q + side
                    fin_out[micro, section] = block[:, side * half : (side + 1) * half]
                    if section < last:
                        pltpu.make_async_remote_copy(
                            src_ref=fin_out.at[micro, section],
                            dst_ref=fin.at[micro],
                            send_sem=fin_send.at[micro],
                            recv_sem=fin_sem.at[micro],
                            device_id=(r, section),
                            device_id_type=MESH,
                        ).start()
                    else:
                        pltpu.make_async_copy(
                            fin_out.at[micro, section], fin.at[micro], fin_sem.at[micro]
                        ).start()

    def relay_turn(t):
        @pl.when((odd == 1) & (t < MICRO))
        def _():
            route(t, 0)

        @pl.when((t >= 1) & (t < MICRO + 1))
        def _():
            apply_section(t - 1)

        @pl.when((odd == 1) & (s < last) & (t >= 2))
        def _():
            route(t - 2, 1)

        @pl.when((odd == 1) & (s < last) & (t == TURNS - 1))
        def _():
            pl.semaphore_signal(done_sem, inc=1, device_id=(r, s - 1), device_id_type=MESH)

        @pl.when((odd == 0) & (s < last - 1) & (t == TURNS - 1))
        def _():
            pl.semaphore_wait(done_sem, 1)

    @pl.when(s == 0)
    def _():
        for micro in range(MICRO):
            for q in range(REPLICAS):
                pltpu.make_async_copy(
                    inputs.at[micro, :, pl.ds(q * SLICE, SLICE)], xbuf.at[micro, q], x_sem.at[micro, q]
                ).start()

    def fetch_piece(piece):
        for which, received in enumerate((received_w, received_m)):
            arrived = received.at[pl.ds(0, 7), pl.ds(0, ROWS)]
            pltpu.make_async_copy(arrived, arrived, rec_sem.at[2 * piece + which]).wait()
            pltpu.make_async_copy(received.at[:, piece_rows(piece)], got.at[which], got_sem.at[which]).start()

    def outer_step(piece):
        for which in range(2):
            here = got.at[which]
            pltpu.make_async_copy(here, here, got_sem.at[which]).wait()

        def block(q, carry):
            rows = slice_rows(q, piece)
            twice_weights = wv[rows, :].astype(jnp.float32) + got[0, q].astype(jnp.float32)
            twice_momentum = near_m[rows, :].astype(jnp.float32) + got[1, q].astype(jnp.float32)
            start_values = near_a[rows, :].astype(jnp.float32)
            delta = start_values - 0.5 * twice_weights
            new_m[rows, :] = (0.45 * twice_momentum + delta).astype(jnp.bfloat16)
            new_w[rows, :] = (start_values - (1.33 * delta + 0.2835 * twice_momentum)).astype(jnp.bfloat16)
            return carry

        lax.fori_loop(0, REPLICAS, block, 0)

    ahead = before_relay(s)
    fill_first, fill_end = beside_relay(odd)

    def advance(u, carry):
        turn = u - ahead

        @pl.when(u == jnp.clip(ahead - 1, 0, STEPS))
        def _():
            load_w.wait()
            wt[...] = wv[...].T

        @pl.when((turn >= 0) & (turn < TURNS))
        def _():
            relay_turn(turn)

        beside = (turn >= fill_first) & (turn < fill_end)
        step = jnp.where(turn < 0, u, jnp.where(turn < TURNS, u - fill_first, u - TURNS + fill_end - fill_first))
        due = ((turn < 0) | (turn >= TURNS) | beside) & (step < 2 * STEPS)

        @pl.when(due & (step >= DEPTH))
        def _():
            sent(step - DEPTH)

        @pl.when(due & (step < STEPS))
        def _():
            take_slices(step)

        @pl.when(due & (step >= STEPS))
        def _():
            pass_on(step - STEPS)

        @pl.when(u == STEPS)
        def _():
            load_m.start()
            load_a.start()

        @pl.when(u == STEPS + 4)
        def _():
            load_m.wait()
            load_a.wait()

        received_now = step - STEPS - DEPTH

        @pl.when(due & (received_now >= 1) & (lax.rem(step, 2) == 0))
        def _():
            fetch_piece(lax.div(received_now - 1, 2))

        @pl.when(due & (received_now >= 2) & (lax.rem(step, 2) == 1))
        def _():
            outer_step(lax.div(received_now - 2, 2))

        return carry

    lax.fori_loop(0, 2 * STEPS + TURNS, advance, 0)
    sent(2 * STEPS - 3)
    fetch_piece(PIECES - 2)
    outer_step(PIECES - 2)
    sent(2 * STEPS - 2)
    sent(2 * STEPS - 1)
    fetch_piece(PIECES - 1)
    outer_step(PIECES - 1)

    def drain(micro, carry):
        eight, seven = obuf.at[micro], obuf.at[micro, pl.ds(0, 7)]

        @pl.when(odd == 0)
        def _():
            pltpu.make_async_copy(eight, eight, o_sem.at[micro]).wait()

        @pl.when(odd == 1)
        def _():
            pltpu.make_async_copy(seven, seven, p2_sem.at[micro, 0]).wait()

        @pl.when((odd == 1) & (s < last))
        def _():
            pltpu.make_async_copy(seven, seven, o_sem.at[micro]).wait()
            pltpu.make_async_copy(eight, eight, p2_sem.at[micro, 1]).wait()

        @pl.when(s == last)
        def _():
            others = fin_out.at[micro, pl.ds(0, last)]
            pltpu.make_async_copy(others, others, fin_send.at[micro]).wait()

        here = fin.at[micro]
        pltpu.make_async_copy(here, here, fin_sem.at[micro]).wait()
        finals[micro] = fin[micro]
        return carry

    lax.fori_loop(0, MICRO, drain, 0)


def relay_and_exchange(inputs, routes, partner, weights, momentum, anchor):
    bf16 = jnp.bfloat16
    dma = pltpu.SemaphoreType.DMA
    whole = pl.BlockSpec(memory_space=pltpu.VMEM)
    scalars = pl.BlockSpec(memory_space=pltpu.SMEM)
    far_off = pl.BlockSpec(memory_space=pltpu.HBM)
    return pl.pallas_call(
        kernel,
        out_shape=(
            jax.ShapeDtypeStruct((MICRO, TOKENS, WIDTH // SECTIONS), bf16),
            jax.ShapeDtypeStruct((2, REPLICAS, SLICE, HIDDEN), bf16),
            jax.ShapeDtypeStruct((REPLICAS, SLICE, HIDDEN), bf16),
            jax.ShapeDtypeStruct((REPLICAS, SLICE, HIDDEN), bf16),
            pltpu.VMEM((WIDTH, HIDDEN), bf16),
            pltpu.VMEM((WIDTH, HIDDEN), bf16),
        ),
        in_specs=[far_off, scalars, scalars, far_off, far_off, far_off],
        out_specs=(whole, far_off, far_off, far_off, whole, whole),
        scratch_shapes=[
            pltpu.VMEM((WIDTH, HIDDEN), bf16),
            pltpu.VMEM((WIDTH, HIDDEN), bf16),
            pltpu.VMEM((WIDTH, HIDDEN), bf16),
            pltpu.VMEM((2, REPLICAS, ROWS, HIDDEN), bf16),
            pltpu.VMEM((HIDDEN, WIDTH), bf16),
            pltpu.VMEM((MICRO, REPLICAS, TOKENS, SLICE), bf16),
            pltpu.VMEM((MICRO, REPLICAS, TOKENS, SLICE), bf16),
            pltpu.VMEM((MICRO, 2, REPLICAS, TOKENS, SLICE), bf16),
            pltpu.VMEM((MICRO, 2, REPLICAS, TOKENS, SLICE), bf16),
            pltpu.VMEM((MICRO, TOKENS, WIDTH // SECTIONS), bf16),
            pltpu.VMEM((MICRO, SECTIONS, TOKENS, WIDTH // SECTIONS), bf16),
            pltpu.VMEM((REPLICAS, ROWS, HIDDEN), bf16),
            pltpu.VMEM((DEPTH, REPLICAS, ROWS, HIDDEN), bf16),
            dma,
            dma((MICRO, REPLICAS)),
            dma((MICRO,)),
            dma((MICRO, 2)),
            dma((MICRO, 2)),
            dma((MICRO,)),
            dma((MICRO,)),
            dma((STEPS,)),
            dma((2 * STEPS,)),
            dma((STEPS,)),
            dma((STEPS,)),
            dma,
            pltpu.SemaphoreType.REGULAR,
            dma,
            dma,
            dma((2,)),
        ],
        compiler_params=pltpu.CompilerParams(
            collective_id=1, has_side_effects=True, vmem_limit_bytes=55 * 2**20
        ),
        cost_estimate=pl.CostEstimate(
            flops=2**30, bytes_accessed=48 * 2**20, transcendentals=2**16
        ),
        name="relay_and_exchange",
    )(inputs, routes, partner, weights, momentum, anchor)


def body(inputs, routes, weights, anchor, momentum, partner):
    finals, _, _, _, new_weights, new_momentum = relay_and_exchange(
        inputs[0], jnp.swapaxes(routes, 1, 2), partner, weights[0, 0], momentum[0, 0], anchor[0, 0]
    )
    return (finals[None], new_weights[None, None], new_momentum[None, None])


def solution(mesh):
    in_specs = (
        P("replica", None, None, None),
        P(),
        P("replica", "section", None, None),
        P("replica", "section", None, None),
        P("replica", "section", None, None),
        P(),
    )
    out_specs = (
        P("replica", None, None, "section"),
        P("replica", "section", None, None),
        P("replica", "section", None, None),
    )
    return jax.shard_map(body, mesh=mesh, in_specs=in_specs, out_specs=out_specs, check_vma=False)
```

```python
import functools

import jax
import jax.numpy as jnp
from jax import lax
from jax.experimental import pallas as pl
from jax.experimental.pallas import tpu as pltpu
from jax.sharding import PartitionSpec as P

MESH = pl.DeviceIdType.MESH
FAR = (6, 2, 5, 7, 4, 1, 3)
NEAR = (0, 1, 3, 4, 5, 7, 2, 6)
REPLICAS = 8
SECTIONS = 16
MICRO = 4
TOKENS = 32
WIDTH = 4096
HIDDEN = 512
SLICE = WIDTH // REPLICAS
PIECES = 8
ROWS = SLICE // PIECES
STEPS = 2 * PIECES
TURNS = MICRO + 2
DEPTH = 3


def other_replica(r, k):
    x, y = lax.rem(r, 4), lax.div(r, 4)
    x = (x, x + 1 - 2 * lax.rem(x, 2), lax.rem(x + 2, 4), 3 - x)[k % 4]
    y = (y, 1 - y)[k // 4]
    return y * 4 + x


def before_relay(section):
    return 1 + 4 * lax.div(section, 2) + jnp.minimum(lax.div(section, 2), 1) + lax.div(section, 8) + lax.rem(section, 2)


def beside_relay(odd):
    return 5, 5


def kernel(
    inputs, routes, partner, weights, momentum, anchor,
    finals, landed, received_w, received_m, new_w, new_m,
    wv, near_m, near_a, got, wt, xbuf, obuf, first, second, fin, fin_out, stage_in, stage_out,
    w_sem, x_sem, o_sem, p1_sem, p2_sem, fin_sem, fin_send, land_sem, bulk_send, rec_sem, own_sem, stage_sem, done_sem, m_sem, a_sem, got_sem,
):
    r = lax.axis_index("replica")
    s = lax.axis_index("section")
    odd = lax.rem(s, 2)
    last = SECTIONS - 1

    load_w = pltpu.make_async_copy(weights, wv, w_sem)
    load_w.start()
    load_m = pltpu.make_async_copy(momentum, near_m, m_sem)
    load_a = pltpu.make_async_copy(anchor, near_a, a_sem)

    barrier = pltpu.get_barrier_semaphore()

    def greet(device):
        pl.semaphore_signal(barrier, inc=1, device_id=device, device_id_type=MESH)

    for k in range(1, 8):
        greet((other_replica(r, k), s))

    @pl.when(s > 0)
    def _():
        for k in range(8):
            greet((other_replica(r, k), s - 1))

    @pl.when(s < last - 1)
    def _():
        greet((r, last))

    @pl.when((odd == 0) & (s < last - 1))
    def _():
        greet((r, s + 1))

    pl.semaphore_wait(barrier, jnp.where(s < last, 15 + odd, 7 + last - 1))

    def slice_rows(q, piece):
        return pl.ds(pl.multiple_of(q * SLICE + piece * ROWS, ROWS), ROWS)

    def piece_rows(piece):
        return pl.ds(pl.multiple_of(piece * ROWS, ROWS), ROWS)

    def take_slices(step):
        array, piece = lax.rem(step, 2), lax.div(step, 2)
        for which, source in enumerate((weights, momentum)):

            @pl.when(array == which)
            def _():
                for k in FAR:
                    q = other_replica(r, k)
                    pltpu.make_async_remote_copy(
                        src_ref=source.at[slice_rows(q, piece)],
                        dst_ref=landed.at[which, r, piece_rows(piece)],
                        send_sem=bulk_send.at[step],
                        recv_sem=land_sem.at[step],
                        device_id=(q, s),
                        device_id_type=MESH,
                    ).start()
                pltpu.make_async_copy(
                    source.at[slice_rows(r, piece)],
                    landed.at[which, r, piece_rows(piece)],
                    land_sem.at[step],
                ).start()

    def pass_on(step):
        array, piece = lax.rem(step, 2), lax.div(step, 2)
        slot = lax.rem(step, DEPTH)
        arrived = landed.at[array, :, piece_rows(piece)]
        pltpu.make_async_copy(arrived, arrived, land_sem.at[step]).wait()
        fetch = pltpu.make_async_copy(arrived, stage_in, stage_sem)
        fetch.start()
        fetch.wait()
        for k in FAR + (0,):
            d = other_replica(r, k)
            stage_out[slot, d] = stage_in[partner[d]]
        for which, received in enumerate((received_w, received_m)):

            @pl.when(array == which)
            def _():
                for k in FAR:
                    d = other_replica(r, k)
                    pltpu.make_async_remote_copy(
                        src_ref=stage_out.at[slot, d],
                        dst_ref=received.at[r, piece_rows(piece)],
                        send_sem=bulk_send.at[STEPS + step],
                        recv_sem=rec_sem.at[step],
                        device_id=(d, s),
                        device_id_type=MESH,
                    ).start()
                pltpu.make_async_copy(
                    stage_out.at[slot, r],
                    received.at[r, piece_rows(piece)],
                    own_sem.at[step],
                ).start()

    def sent(step):
        some = landed.at[0, pl.ds(0, 7), pl.ds(0, ROWS)]
        pltpu.make_async_copy(some, some, bulk_send.at[step]).wait()

        @pl.when(step >= STEPS)
        def _():
            one = stage_out.at[0, 0]
            pltpu.make_async_copy(one, one, own_sem.at[step - STEPS]).wait()

    def route(micro, way):
        whole = first.at[micro, way]
        pltpu.make_async_copy(whole, whole, p1_sem.at[micro, way]).wait()
        row = s - 1 + way
        targets = [routes[micro, source, row] for source in range(REPLICAS)]
        for k in FAR + (0,):
            d = other_replica(r, k)
            chosen = first[micro, way, 0]
            for source in range(1, REPLICAS):
                chosen = jnp.where(targets[source] == d, first[micro, way, source], chosen)
            second[micro, way, d] = chosen
            passing = functools.partial(
                pltpu.make_async_remote_copy,
                src_ref=second.at[micro, way, d],
                dst_ref=xbuf.at[micro, r],
                send_sem=p2_sem.at[micro, way],
                recv_sem=x_sem.at[micro, r],
                device_id=(d, s + way),
                device_id_type=MESH,
            )
            if k or way:
                passing().start()
            else:
                pltpu.make_async_copy(second.at[micro, way, d], xbuf.at[micro, r], x_sem.at[micro, r]).start()

    def apply_section(micro):
        before = jnp.zeros((TOKENS, HIDDEN), jnp.float32)
        squares = jnp.zeros((TOKENS, 128), jnp.float32)
        for k in NEAR:
            q = other_replica(r, k)
            here = xbuf.at[micro, q]
            pltpu.make_async_copy(here, here, x_sem.at[micro, q]).wait()
            block = xbuf[micro, q]
            rows = pl.ds(pl.multiple_of(q * SLICE, SLICE), SLICE)
            before = before + jnp.dot(block, wv[rows, :], preferred_element_type=jnp.float32)
            values = block.astype(jnp.float32)
            values = values * values
            for c in range(SLICE // 128):
                squares = squares + values[:, c * 128 : (c + 1) * 128]
        factor = lax.rsqrt(jnp.sum(squares, axis=-1, keepdims=True) * (1.0 / WIDTH) + 1e-05)
        before = before * (factor * WIDTH ** (-0.5))
        hidden = jax.nn.silu(before).astype(jnp.bfloat16)

        def leaving(q):
            columns = pl.ds(pl.multiple_of(q * SLICE, SLICE), SLICE)
            branch = jnp.dot(hidden, wt[:, columns], preferred_element_type=jnp.float32)
            return (xbuf[micro, q].astype(jnp.float32) + branch * HIDDEN ** (-0.5)).astype(jnp.bfloat16)

        @pl.when(s < last)
        def _():
            for k in FAR + (0,):
                q = other_replica(r, k)
                obuf[micro, q] = leaving(q)
                remote = pltpu.make_async_remote_copy(
                    src_ref=obuf.at[micro, q],
                    dst_ref=first.at[micro, odd, r],
                    send_sem=o_sem.at[micro],
                    recv_sem=p1_sem.at[micro, odd],
                    device_id=(q, s + 1 - odd),
                    device_id_type=MESH,
                )
                if k:
                    remote.start()
                else:
                    pl.when(odd == 0)(remote.start)

                    @pl.when(odd == 1)
                    def _():
                        pltpu.make_async_copy(
                            obuf.at[micro, q], first.at[micro, 1, r], p1_sem.at[micro, 1]
                        ).start()

        @pl.when(s == last)
        def _():
            half = SLICE // 2
            for q in range(REPLICAS):
                block = leaving(q)
                for side in range(2):
                    section = 2 * q + side
                    fin_out[micro, section] = block[:, side * half : (side + 1) * half]
                    if section < last:
                        pltpu.make_async_remote_copy(
                            src_ref=fin_out.at[micro, section],
                            dst_ref=fin.at[micro],
                            send_sem=fin_send.at[micro],
                            recv_sem=fin_sem.at[micro],
                            device_id=(r, section),
                            device_id_type=MESH,
                        ).start()
                    else:
                        pltpu.make_async_copy(
                            fin_out.at[micro, section], fin.at[micro], fin_sem.at[micro]
                        ).start()

    def relay_turn(t):
        @pl.when((odd == 1) & (t < MICRO))
        def _():
            route(t, 0)

        @pl.when((t >= 1) & (t < MICRO + 1))
        def _():
            apply_section(t - 1)

        @pl.when((odd == 1) & (s < last) & (t >= 2))
        def _():
            route(t - 2, 1)

        @pl.when((odd == 1) & (s < last) & (t == TURNS - 1))
        def _():
            pl.semaphore_signal(done_sem, inc=1, device_id=(r, s - 1), device_id_type=MESH)

        @pl.when((odd == 0) & (s < last - 1) & (t == TURNS - 1))
        def _():
            pl.semaphore_wait(done_sem, 1)

    @pl.when(s == 0)
    def _():
        for micro in range(MICRO):
            for q in range(REPLICAS):
                pltpu.make_async_copy(
                    inputs.at[micro, :, pl.ds(q * SLICE, SLICE)], xbuf.at[micro, q], x_sem.at[micro, q]
                ).start()

    def fetch_piece(piece):
        for which, received in enumerate((received_w, received_m)):
            arrived = received.at[pl.ds(0, 7), pl.ds(0, ROWS)]
            pltpu.make_async_copy(arrived, arrived, rec_sem.at[2 * piece + which]).wait()
            pltpu.make_async_copy(received.at[:, piece_rows(piece)], got.at[which], got_sem.at[which]).start()

    def outer_step(piece):
        for which in range(2):
            here = got.at[which]
            pltpu.make_async_copy(here, here, got_sem.at[which]).wait()

        def block(q, carry):
            rows = slice_rows(q, piece)
            twice_weights = wv[rows, :].astype(jnp.float32) + got[0, q].astype(jnp.float32)
            twice_momentum = near_m[rows, :].astype(jnp.float32) + got[1, q].astype(jnp.float32)
            start_values = near_a[rows, :].astype(jnp.float32)
            delta = start_values - 0.5 * twice_weights
            new_m[rows, :] = (0.45 * twice_momentum + delta).astype(jnp.bfloat16)
            new_w[rows, :] = (start_values - (1.33 * delta + 0.2835 * twice_momentum)).astype(jnp.bfloat16)
            return carry

        lax.fori_loop(0, REPLICAS, block, 0)

    ahead = before_relay(s)
    fill_first, fill_end = beside_relay(odd)

    def advance(u, carry):
        turn = u - ahead

        @pl.when(u == jnp.clip(ahead - 1, 0, STEPS))
        def _():
            load_w.wait()
            wt[...] = wv[...].T

        @pl.when((turn >= 0) & (turn < TURNS))
        def _():
            relay_turn(turn)

        beside = (turn >= fill_first) & (turn < fill_end)
        step = jnp.where(turn < 0, u, jnp.where(turn < TURNS, u - fill_first, u - TURNS + fill_end - fill_first))
        due = ((turn < 0) | (turn >= TURNS) | beside) & (step < 2 * STEPS)

        @pl.when(due & (step >= DEPTH))
        def _():
            sent(step - DEPTH)

        @pl.when(due & (step < STEPS))
        def _():
            take_slices(step)

        @pl.when(due & (step >= STEPS))
        def _():
            pass_on(step - STEPS)

        @pl.when(u == STEPS)
        def _():
            load_m.start()
            load_a.start()

        @pl.when(u == STEPS + 4)
        def _():
            load_m.wait()
            load_a.wait()

        received_now = step - STEPS - DEPTH

        @pl.when(due & (received_now >= 1) & (lax.rem(step, 2) == 0))
        def _():
            fetch_piece(lax.div(received_now - 1, 2))

        @pl.when(due & (received_now >= 2) & (lax.rem(step, 2) == 1))
        def _():
            outer_step(lax.div(received_now - 2, 2))

        return carry

    lax.fori_loop(0, 2 * STEPS + TURNS, advance, 0)
    sent(2 * STEPS - 3)
    fetch_piece(PIECES - 2)
    outer_step(PIECES - 2)

    def drain(micro, carry):
        eight, seven = obuf.at[micro], obuf.at[micro, pl.ds(0, 7)]

        @pl.when(odd == 0)
        def _():
            pltpu.make_async_copy(eight, eight, o_sem.at[micro]).wait()

        @pl.when(odd == 1)
        def _():
            pltpu.make_async_copy(seven, seven, p2_sem.at[micro, 0]).wait()

        @pl.when((odd == 1) & (s < last))
        def _():
            pltpu.make_async_copy(seven, seven, o_sem.at[micro]).wait()
            pltpu.make_async_copy(eight, eight, p2_sem.at[micro, 1]).wait()

        @pl.when(s == last)
        def _():
            others = fin_out.at[micro, pl.ds(0, last)]
            pltpu.make_async_copy(others, others, fin_send.at[micro]).wait()

        here = fin.at[micro]
        pltpu.make_async_copy(here, here, fin_sem.at[micro]).wait()
        finals[micro] = fin[micro]
        return carry

    lax.fori_loop(0, MICRO, drain, 0)

    sent(2 * STEPS - 2)
    sent(2 * STEPS - 1)
    fetch_piece(PIECES - 1)
    outer_step(PIECES - 1)


def relay_and_exchange(inputs, routes, partner, weights, momentum, anchor):
    bf16 = jnp.bfloat16
    dma = pltpu.SemaphoreType.DMA
    whole = pl.BlockSpec(memory_space=pltpu.VMEM)
    scalars = pl.BlockSpec(memory_space=pltpu.SMEM)
    far_off = pl.BlockSpec(memory_space=pltpu.HBM)
    return pl.pallas_call(
        kernel,
        out_shape=(
            pltpu.VMEM((MICRO, TOKENS, WIDTH // SECTIONS), bf16),
            jax.ShapeDtypeStruct((2, REPLICAS, SLICE, HIDDEN), bf16),
            jax.ShapeDtypeStruct((REPLICAS, SLICE, HIDDEN), bf16),
            jax.ShapeDtypeStruct((REPLICAS, SLICE, HIDDEN), bf16),
            pltpu.VMEM((WIDTH, HIDDEN), bf16),
            pltpu.VMEM((WIDTH, HIDDEN), bf16),
        ),
        in_specs=[far_off, scalars, scalars, far_off, far_off, far_off],
        out_specs=(whole, far_off, far_off, far_off, whole, whole),
        scratch_shapes=[
            pltpu.VMEM((WIDTH, HIDDEN), bf16),
            pltpu.VMEM((WIDTH, HIDDEN), bf16),
            pltpu.VMEM((WIDTH, HIDDEN), bf16),
            pltpu.VMEM((2, REPLICAS, ROWS, HIDDEN), bf16),
            pltpu.VMEM((HIDDEN, WIDTH), bf16),
            pltpu.VMEM((MICRO, REPLICAS, TOKENS, SLICE), bf16),
            pltpu.VMEM((MICRO, REPLICAS, TOKENS, SLICE), bf16),
            pltpu.VMEM((MICRO, 2, REPLICAS, TOKENS, SLICE), bf16),
            pltpu.VMEM((MICRO, 2, REPLICAS, TOKENS, SLICE), bf16),
            pltpu.VMEM((MICRO, TOKENS, WIDTH // SECTIONS), bf16),
            pltpu.VMEM((MICRO, SECTIONS, TOKENS, WIDTH // SECTIONS), bf16),
            pltpu.VMEM((REPLICAS, ROWS, HIDDEN), bf16),
            pltpu.VMEM((DEPTH, REPLICAS, ROWS, HIDDEN), bf16),
            dma,
            dma((MICRO, REPLICAS)),
            dma((MICRO,)),
            dma((MICRO, 2)),
            dma((MICRO, 2)),
            dma((MICRO,)),
            dma((MICRO,)),
            dma((STEPS,)),
            dma((2 * STEPS,)),
            dma((STEPS,)),
            dma((STEPS,)),
            dma,
            pltpu.SemaphoreType.REGULAR,
            dma,
            dma,
            dma((2,)),
        ],
        compiler_params=pltpu.CompilerParams(
            collective_id=1, has_side_effects=True, vmem_limit_bytes=55 * 2**20
        ),
        cost_estimate=pl.CostEstimate(
            flops=2**30, bytes_accessed=48 * 2**20, transcendentals=2**16
        ),
        name="relay_and_exchange",
    )(inputs, routes, partner, weights, momentum, anchor)


def body(inputs, routes, weights, anchor, momentum, partner):
    finals, _, _, _, new_weights, new_momentum = relay_and_exchange(
        inputs[0], jnp.swapaxes(routes, 1, 2), partner, weights[0, 0], momentum[0, 0], anchor[0, 0]
    )
    return (finals[None], new_weights[None, None], new_momentum[None, None])


def solution(mesh):
    in_specs = (
        P("replica", None, None, None),
        P(),
        P("replica", "section", None, None),
        P("replica", "section", None, None),
        P("replica", "section", None, None),
        P(),
    )
    out_specs = (
        P("replica", None, None, "section"),
        P("replica", "section", None, None),
        P("replica", "section", None, None),
    )
    return jax.shard_map(body, mesh=mesh, in_specs=in_specs, out_specs=out_specs, check_vma=False)
```
